512 devices in a mesh: seq: 128 (over z, y, x_hi), ch: 4 (over x_lo, core).
Axes of the slice: x: 4 (x_hi: 2, x_lo: 2; x = x_hi * 2 + x_lo), y: 8, z: 8, core: 2. Of those that a mesh axis runs over, the one named last changes fastest.
Arguments:
- tokens: bfloat16 [32768, 1024], P('seq', 'ch'), may hold values from -24 to 24
- cotangent: bfloat16 [32768, 1024], P('seq', 'ch'), may hold values from -6 to 6
- first_factor: bfloat16 [16, 64, 64], replicated, may hold values from -0.75 to 0.75
- second_factor: bfloat16 [64, 16, 16], replicated, may hold values from -1.5 to 1.5
- third_factor: bfloat16 [64, 32, 32], replicated, may hold values from -1 to 1
- gate_weight: bfloat16 [1024, 1024], P(None, 'ch'), may hold values from -0.1875 to 0.1875
Outputs:
- output: bfloat16 [32768, 1024], P('seq', 'ch')
- input_grad: bfloat16 [32768, 1024], P('seq', 'ch')
- first_grad: bfloat16 [16, 64, 64], replicated
- second_grad: bfloat16 [64, 16, 16], replicated
- third_grad: bfloat16 [64, 32, 32], replicated
- gate_grad: float32 [1024, 1024], P('seq', 'ch')
The draws below stay inside these ranges and needn't reach their ends.
All inputs are finite; a program needn't handle non-finite values.
Results may differ from the reference program's by a relative error of at most 0.0068.
Values may be sent and summed in bfloat16 or wider, within the bound.
A program may use at most 64 MiB of HBM per device.

```python
import jax
import jax.numpy as jnp

A = 32
B = 16
C = 64
D = 1024
L = 32768


def spiked(result, stream_key, source, target, blocks, factor):
    def block_of(axis_at):
        return (jnp.arange(result.shape[axis_at]) // (result.shape[axis_at] // blocks)).reshape((-1,) + (1,) * (result.ndim - 1 - axis_at))

    near = jax.random.permutation(stream_key, blocks)[block_of(target)]
    second = (block_of(target) + blocks // 2) % blocks
    return jnp.where((block_of(source) == near) | (block_of(source) == second), factor * result, result)


def levels(rng, shape, split, low, top_value):
    loudness, own = 1.0, jax.random.fold_in(rng, 6)
    for position, parts in split:
        draws = jnp.exp(jax.random.uniform(jax.random.fold_in(own, position), (parts,), jnp.float32, low / len(split), top_value / len(split)))
        loudness = loudness * jnp.repeat(draws, shape[position] // parts).reshape([-1 if axis == position else 1 for axis in range(len(shape))])
    return loudness


def noise(own_key, extent, width, most, shards=(), held_as=jnp.bfloat16):
    array = width * jax.random.normal(own_key, extent, jnp.float32)
    if shards:
        array = array * levels(own_key, extent, shards, -0.22, 0.18)
    return jnp.clip(array, -most, most).astype(held_as)


def gaussian_with(stream_key, dims, deviation, limit, shards, heavy, held_as=jnp.bfloat16):
    entries = deviation * jax.random.normal(stream_key, dims, jnp.float32)
    if shards:
        entries = entries * levels(stream_key, dims, shards, -0.22, 0.18)
    return jnp.clip(spiked(entries, jax.random.fold_in(stream_key, 3), *heavy), -limit, limit).astype(held_as)


def setup_inputs(seed: int = 0) -> dict:
    splits = jax.random.split(jax.random.key(seed), 7)
    return {
        "tokens": gaussian_with(splits[0], (L, D), 1.0, 24.0, ((0, 128), (1, 4)), (0, 1, 128, 5.5)),
        "cotangent": noise(splits[1], (L, D), 1.0, 6.0, ((0, 128), (1, 4))),
        "first_factor": noise(splits[2], (B, C, C), C ** -0.5, 0.75),
        "second_factor": noise(splits[3], (C, B, B), B ** -0.5, 1.5),
        "third_factor": noise(splits[4], (C, A, A), A ** -0.5, 1.0),
        "gate_weight": noise(splits[5], (D, D), D ** -0.5, 0.1875, ((1, 4),)),
    }


def reference(tokens, cotangent, first_factor, second_factor, third_factor, gate_weight):
    grid_in = tokens.reshape(A, B, C, D).astype(jnp.float32)
    first_w = first_factor.astype(jnp.float32)
    second_w = second_factor.astype(jnp.float32)
    third_w = third_factor.astype(jnp.float32)
    mixed_first = jnp.einsum("bcd,abdh->abch", first_w, grid_in).astype(jnp.bfloat16)
    mixed_second = jnp.einsum("cbe,aech->abch", second_w, mixed_first.astype(jnp.float32)).astype(jnp.bfloat16)
    mixed = jnp.einsum("cae,ebch->abch", third_w, mixed_second.astype(jnp.float32)).astype(jnp.bfloat16)
    mixed_flat = mixed.reshape(L, D).astype(jnp.float32)
    gate_pre = jnp.dot(tokens, gate_weight, preferred_element_type=jnp.float32)
    sigmoid_gate = jax.nn.sigmoid(gate_pre)
    activation = gate_pre * sigmoid_gate
    output = (tokens.astype(jnp.float32) + mixed_flat * activation).astype(jnp.bfloat16)
    upstream = cotangent.astype(jnp.float32)
    mix_grad = (upstream * activation).astype(jnp.bfloat16)
    pre_grad = (upstream * mixed_flat * sigmoid_gate * (1.0 + gate_pre * (1.0 - sigmoid_gate))).astype(jnp.bfloat16)
    grad_grid = mix_grad.reshape(A, B, C, D).astype(jnp.float32)
    back_second = jnp.einsum("cae,abch->ebch", third_w, grad_grid).astype(jnp.bfloat16)
    third_grad = jnp.einsum("abch,ebch->cae", grad_grid, mixed_second.astype(jnp.float32))
    back_first = jnp.einsum("cbe,abch->aech", second_w, back_second.astype(jnp.float32)).astype(jnp.bfloat16)
    second_grad = jnp.einsum("abch,aech->cbe", back_second.astype(jnp.float32), mixed_first.astype(jnp.float32))
    mix_input = jnp.einsum("bcd,abch->abdh", first_w, back_first.astype(jnp.float32)).reshape(L, D)
    first_grad = jnp.einsum("abch,abdh->bcd", back_first.astype(jnp.float32), grid_in)
    gate_input = jnp.dot(pre_grad, gate_weight.T, preferred_element_type=jnp.float32)
    gate_grad = jnp.dot(tokens.T, pre_grad, preferred_element_type=jnp.float32)
    input_grad = (upstream + mix_input + gate_input).astype(jnp.bfloat16)
    return (output, input_grad, first_grad.astype(jnp.bfloat16), second_grad.astype(jnp.bfloat16),
            third_grad.astype(jnp.bfloat16), gate_grad)
```

```python
import jax
import jax.numpy as jnp
from jax import lax
from jax.sharding import Mesh
from jax.sharding import PartitionSpec as P
from jax.experimental import pallas as pl
from jax.experimental.pallas import tpu as pltpu

A = 32
B = 16
C = 64
SEQ = ("seq_0", "seq_1", "seq_2")
SEQ_CH = ("seq_0", "seq_1", "seq_2", "ch")


def seq_peer(step):
    me = lax.axis_index(SEQ)
    peer = lax.rem(me + step, 128)
    where = {"seq_0": peer // 16, "seq_1": lax.rem(peer // 2, 8), "seq_2": lax.rem(peer, 2)}
    return me, peer, where


def exchange_kernel(x_ref, out_ref, send_sem, recv_sem):
    barrier = pltpu.get_barrier_semaphore()

    def greet(step, carry):
        pl.semaphore_signal(
            barrier, inc=1, device_id=seq_peer(step)[2], device_id_type=pl.DeviceIdType.MESH
        )
        return carry

    lax.fori_loop(1, 128, greet, 0)
    me = lax.axis_index(SEQ)
    out_ref[pl.ds(me, 1)] = x_ref[pl.ds(me, 1)]
    pl.semaphore_wait(barrier, 127)

    def send(step, carry):
        me, peer, where = seq_peer(step)
        pltpu.make_async_remote_copy(
            x_ref.at[peer],
            out_ref.at[me],
            send_sem,
            recv_sem,
            device_id=where,
            device_id_type=pl.DeviceIdType.MESH,
        ).start()
        return carry

    lax.fori_loop(1, 128, send, 0)
    part = out_ref.at[pl.ds(0, 127)]
    pltpu.make_async_copy(part, part, send_sem).wait()
    pltpu.make_async_copy(part, part, recv_sem).wait()


def exchange(x):
    return pl.pallas_call(
        exchange_kernel,
        out_shape=jax.ShapeDtypeStruct(x.shape, x.dtype),
        in_specs=[pl.BlockSpec(memory_space=pltpu.VMEM)],
        out_specs=pl.BlockSpec(memory_space=pltpu.VMEM),
        scratch_shapes=[pltpu.SemaphoreType.DMA, pltpu.SemaphoreType.DMA],
        compiler_params=pltpu.CompilerParams(collective_id=0, has_side_effects=True),
    )(x)


def sent_together(arrays, axis, dim, along):
    both = jnp.concatenate(arrays, axis=along)
    out, at, outs = (lax.all_gather(both, axis, axis=dim, tiled=True), 0, [])
    for a in arrays:
        outs.append(lax.slice_in_dim(out, at, at + a.shape[along], axis=along))
        at += a.shape[along]
    return tuple(outs)


def joined_along(blocks, dim):
    blocks = jnp.moveaxis(blocks, 0, dim)
    lengths = blocks.shape
    return blocks.reshape(*lengths[:dim], lengths[dim] * lengths[dim + 1], *lengths[dim + 2 :])


def sent_to_all(x, axis):
    copies = jnp.broadcast_to(x, (lax.axis_size(axis), *x.shape))
    return lax.all_to_all(copies, axis, split_axis=0, concat_axis=0, tiled=True)


def collect(x, axis, dim):
    return joined_along(sent_to_all(x, axis), dim)


def sum_by_axis(total, axes):
    for axis in axes:
        total = lax.psum_scatter(total, axis, scatter_dimension=0, tiled=True)
    return total


def on_device(tokens, cotangent, first_factor, second_factor, third_factor, gate_weight):
    seq_count = lax.axis_size(SEQ)
    seq_index = lax.axis_index(SEQ)
    per_device_c = max(1, C // seq_count)
    splits = max(1, seq_count // C)
    local_rows, width = tokens.shape
    narrow = width // splits
    blocks = local_rows // C
    batch_b = min(blocks, B)
    start_b = seq_index * blocks % B
    first_sel = lax.dynamic_slice_in_dim(first_factor, start_b, blocks, 0)
    column = seq_index // splits * per_device_c
    second_sel = lax.dynamic_slice_in_dim(second_factor, column, per_device_c, 0)
    third_sel = lax.dynamic_slice_in_dim(third_factor, column, per_device_c, 0)
    grid_view = tokens.reshape(blocks // batch_b, batch_b, C, width)
    mixed_first = jnp.einsum(
        "bcd,ibdh->ibch", first_sel, grid_view, preferred_element_type=jnp.float32
    ).astype(jnp.bfloat16)

    def spread(values):
        return jnp.swapaxes(values.reshape(blocks, seq_count, narrow), 0, 1)

    def home(values):
        return jnp.swapaxes(exchange(values.reshape(seq_count, blocks, narrow)), 0, 1)

    received = exchange(spread(mixed_first))
    item_count = received.shape[2]
    far_view = received.reshape(A, B, per_device_c, item_count)
    second_val = jnp.einsum(
        "kbe,aekh->abkh", second_sel, far_view, preferred_element_type=jnp.float32
    ).astype(jnp.bfloat16)
    third_val = jnp.einsum(
        "kae,ebkh->abkh", third_sel, second_val, preferred_element_type=jnp.float32
    ).astype(jnp.bfloat16)
    first_far = received
    second_far = second_val.reshape(A * B, 1, per_device_c, item_count)
    mixed_far = third_val.reshape(A * B, 1, per_device_c, item_count)
    mixed_back = home(mixed_far).reshape(
        local_rows, width
    )
    full_tokens, full_weight = sent_together((tokens, gate_weight), "ch", 1, 0)
    own_rows = lax.dynamic_slice_in_dim(full_weight, lax.axis_index("ch") * width, width, 0)
    gate_pre = jnp.dot(full_tokens, gate_weight, preferred_element_type=jnp.float32)
    sigmoid_gate = jax.nn.sigmoid(gate_pre)
    activation = gate_pre * sigmoid_gate
    mixed_float = mixed_back.astype(jnp.float32)
    output = (tokens.astype(jnp.float32) + mixed_float * activation).astype(jnp.bfloat16)
    upstream = cotangent.astype(jnp.float32)
    mix_grad = (upstream * activation).astype(jnp.bfloat16)
    pre_grad = (
        upstream * mixed_float * sigmoid_gate * (1.0 + gate_pre * (1.0 - sigmoid_gate))
    ).astype(jnp.bfloat16)
    received = exchange(spread(mix_grad))
    item_count = received.shape[2]
    far_view = received.reshape(A, B, per_device_c, item_count)
    back_second = jnp.einsum(
        "kae,abkh->ebkh", third_sel, far_view, preferred_element_type=jnp.float32
    ).astype(jnp.bfloat16)
    back_first = jnp.einsum(
        "kbe,abkh->aekh", second_sel, back_second, preferred_element_type=jnp.float32
    ).astype(jnp.bfloat16)
    second_back = back_second.reshape(A * B, 1, per_device_c, item_count)
    first_back = back_first.reshape(A * B, 1, per_device_c, item_count)
    third_part = jnp.einsum(
        "abkh,ebkh->kae",
        received.reshape(A, B, per_device_c, narrow),
        second_far.reshape(A, B, per_device_c, narrow),
        preferred_element_type=jnp.float32,
    )
    second_part = jnp.einsum(
        "abkh,aekh->kbe",
        second_back.reshape(A, B, per_device_c, narrow),
        first_far.reshape(A, B, per_device_c, narrow),
        preferred_element_type=jnp.float32,
    )
    first_home = home(first_back).reshape(
        blocks // batch_b, batch_b, C, width
    )
    mix_input = jnp.einsum(
        "bcd,ibch->ibdh", first_sel, first_home, preferred_element_type=jnp.float32
    ).reshape(local_rows, width)
    first_part = jnp.einsum(
        "ibch,ibdh->bcd", first_home, grid_view, preferred_element_type=jnp.float32
    )
    first_full = lax.dynamic_update_slice_in_dim(
        jnp.zeros((B, C, C), jnp.float32), first_part, start_b, 0
    )
    second_full = lax.dynamic_update_slice_in_dim(
        jnp.zeros((C, B, B), jnp.float32), second_part, column, 0
    )
    third_full = lax.dynamic_update_slice_in_dim(
        jnp.zeros((C, A, A), jnp.float32), third_part, column, 0
    )
    first_sum, second_sum, third_sum = lax.psum((first_full, second_full, third_full), SEQ_CH)
    gate_input = lax.dot_general(
        collect(pre_grad, "ch", 1),
        own_rows,
        (((1,), (1,)), ((), ())),
        preferred_element_type=jnp.float32,
    )
    gate_grad = sum_by_axis(
        lax.dot_general(
            full_tokens, pre_grad, (((0,), (0,)), ((), ())), preferred_element_type=jnp.float32
        ),
        SEQ,
    )
    input_grad = (upstream + mix_input + gate_input).astype(jnp.bfloat16)
    return (
        output,
        input_grad,
        first_sum.astype(jnp.bfloat16),
        second_sum.astype(jnp.bfloat16),
        third_sum.astype(jnp.bfloat16),
        gate_grad,
    )


def solution(mesh):
    torus = Mesh(mesh.devices.reshape(8, 8, 2, mesh.shape["ch"]), ("seq_0", "seq_1", "seq_2", "ch"))
    return jax.shard_map(
        on_device,
        mesh=torus,
        in_specs=(P(SEQ, "ch"), P(SEQ, "ch"), P(), P(), P(), P(None, "ch")),
        out_specs=(P(SEQ, "ch"), P(SEQ, "ch"), P(), P(), P(), P(SEQ, "ch")),
        check_vma=False,
    )
```

```python
import jax
import jax.numpy as jnp
from jax import lax
from jax.experimental import pallas as pl
from jax.experimental.pallas import tpu as pltpu
from jax.sharding import Mesh
from jax.sharding import PartitionSpec as P

A = 32
B = 16
C = 64
N = 128
SEQ = ("seq_0", "seq_1", "seq_2")
BF = jnp.bfloat16
F32 = jnp.float32
(TOK, FIRST, WROW, GRAD, MIXED, BACK, PRE, GATE, FG_SUM, FG_CH, FG_ALL, ST_X, ST_CH, ST_ALL) = range(14)


def place(s):
    return {"seq_0": s // 16, "seq_1": lax.rem(s // 2, 8), "seq_2": lax.rem(s, 2)}


def nn(x, y):
    return jnp.dot(x, y, preferred_element_type=F32)


def nt(x, y):
    return lax.dot_general(x, y, (((1,), (1,)), ((), ())), preferred_element_type=F32)


def tn(x, y):
    return lax.dot_general(x, y, (((0,), (0,)), ((), ())), preferred_element_type=F32)


def index(shape, dim):
    return lax.broadcasted_iota(jnp.int32, shape, dim)


def one_hot(flags):
    return jnp.where(flags, 1.0, 0.0).astype(BF)


def summed(x, ones):
    high = x.astype(BF)
    low = (x - high.astype(F32)).astype(BF)
    return nn(high, ones) + nn(low, ones)


def kernel(
    tok_ref, cot_ref, first_ref, second_ref, third_ref, w_ref,
    out_ref, ig_ref, gg_ref, fg_ref, st_ref,
    tok_all, tok_t, w_rows, pre_all,
    first_out, first_in, grad_out, grad_in, mixed_out, mixed_in, back_out, back_in,
    second_val, gate_out, gate_in, fg_out, fg_in, fg_ch, fg_fin, st_x, st_ch, st_fin,
    send_sem, recv_sem,
):
    me = lax.axis_index(SEQ)
    ch = lax.axis_index("ch")
    far, half = me // 2, lax.rem(me, 2)
    row, group = me // 4, lax.rem(me, 4)

    def copy(kind, src, dst, where):
        pltpu.make_async_remote_copy(
            src, dst, send_sem.at[kind], recv_sem.at[kind],
            device_id=where, device_id_type=pl.DeviceIdType.MESH,
        ).start()

    def received(kind, part):
        pltpu.make_async_copy(part, part, recv_sem.at[kind]).wait()

    def sent(kind, part):
        pltpu.make_async_copy(part, part, send_sem.at[kind]).wait()

    def to_seq(kind, src, dst):
        def step(d, carry):
            peer = lax.rem(me + d, N)
            copy(kind, src(peer), dst, place(peer))
            return carry

        lax.fori_loop(1, N, step, 0)

    def to_ch(kind, src, dst):
        for d in (1, 2, 3):
            peer = lax.rem(ch + d, 4)
            copy(kind, src(peer), dst, {"ch": peer})

    barrier = pltpu.get_barrier_semaphore()

    def greet(d, carry):
        pl.semaphore_signal(
            barrier, inc=1, device_id=place(lax.rem(me + d, N)), device_id_type=pl.DeviceIdType.MESH
        )
        return carry

    lax.fori_loop(1, N, greet, 0)
    for d in (1, 2, 3):
        pl.semaphore_signal(
            barrier, inc=1, device_id={"ch": lax.rem(ch + d, 4)}, device_id_type=pl.DeviceIdType.MESH
        )

    square = (256, 256)
    r, k = index(square, 0), index(square, 1)
    to_far = one_hot(k == (r & 3) * 64 + (r >> 2))
    to_home = one_hot(k == (r & 63) * 4 + (r >> 6))
    firsts = [first_ref[group * 4 + b] for b in range(4)]
    mixed_first = jnp.concatenate(
        [nn(firsts[b], tok_ref[b * 64 : b * 64 + 64, :]).astype(BF) for b in range(4)], axis=0
    )

    def split_columns(values, buffer):
        ordered = nn(to_far, values).astype(BF)
        for h in range(2):
            buffer[h] = ordered[:, h * 128 : h * 128 + 128].reshape(C, 4, 128)

    def join_columns(buffer):
        return jnp.concatenate([buffer[h].reshape(256, 128) for h in range(2)], axis=1)

    split_columns(mixed_first, first_out)
    first_in[me] = first_out[half, far]
    tok_all[ch] = tok_ref[...]
    w_rows[ch] = w_ref[pl.ds(pl.multiple_of(ch * 256, 256), 256), :]

    own_second, own_third = second_ref[far], third_ref[far]
    rows32 = one_hot((index((512, 32), 0) >> 4) == index((512, 32), 1))
    rows16 = one_hot((index(square[:1] + (16,), 0) & 15) == index(square[:1] + (16,), 1))
    same_a = (r >> 4) == (k >> 4)
    same_b = (index((512, 512), 0) & 15) == (index((512, 512), 1) & 15)

    def spread_third(t):
        return jnp.where(same_b, nt(t.astype(BF), rows32), 0.0).astype(BF)

    def spread_second(t):
        return jnp.where(same_a, nt(t.astype(BF), rows16), 0.0).astype(BF)

    third_mat, third_back = spread_third(nn(rows32, own_third)), spread_third(nt(rows32, own_third))
    second_mat = spread_second(nn(rows16, own_second))
    second_back = spread_second(nt(rows16, own_second))

    pl.semaphore_wait(barrier, N + 2)

    to_ch(TOK, lambda peer: tok_ref, tok_all.at[ch])
    to_seq(FIRST, lambda peer: first_out.at[lax.rem(peer, 2), peer // 2], first_in.at[me])
    to_ch(WROW, lambda peer: w_ref.at[pl.ds(pl.multiple_of(peer * 256, 256), 256), :], w_rows.at[ch])

    received(TOK, tok_all.at[pl.ds(0, 3)])
    gate = nn(tok_all[0], w_ref[0:256, :])
    for p in range(1, 4):
        gate += nn(tok_all[p], w_ref[p * 256 : p * 256 + 256, :])
    sigmoid = jax.nn.sigmoid(gate)
    activation = gate * sigmoid
    upstream = cot_ref[...].astype(F32)
    split_columns((upstream * activation).astype(BF), grad_out)
    grad_in[me] = grad_out[half, far]
    to_seq(GRAD, lambda peer: grad_out.at[lax.rem(peer, 2), peer // 2], grad_in.at[me])
    for p in range(4):
        tok_t[p] = tok_all[p].T

    received(FIRST, first_in.at[pl.ds(0, N - 1)])
    far_first = first_in[...].reshape(512, 128)
    for h in range(2):
        second_val[h * 256 : h * 256 + 256, :] = nn(second_mat, far_first[h * 256 : h * 256 + 256]).astype(BF)
    mixed_out[...] = nn(third_mat, second_val[...]).astype(BF).reshape(N, 4, 128)
    mixed_in[half, far] = mixed_out[me]
    to_seq(MIXED, lambda peer: mixed_out.at[peer], mixed_in.at[half, far])

    received(GRAD, grad_in.at[pl.ds(0, N - 1)])
    far_grad = grad_in[...].reshape(512, 128)
    back_second = nn(third_back, far_grad).astype(BF)
    back_first = jnp.concatenate(
        [nn(second_back, back_second[h * 256 : h * 256 + 256]).astype(BF) for h in range(2)], axis=0
    )
    back_out[...] = back_first.reshape(N, 4, 128)
    back_in[half, far] = back_out[me]
    to_seq(BACK, lambda peer: back_out.at[peer], back_in.at[half, far])

    third_part = jnp.where(same_b, nt(far_grad, second_val[...]), 0.0)
    third_part = summed(jnp.sum(third_part.reshape(A, B, 512), axis=1), rows32)
    second_part = jnp.zeros((16, 256), F32)
    for h in range(2):
        rows = slice(h * 256, h * 256 + 256)
        term = jnp.where(same_a, nt(back_second[rows], far_first[rows]), 0.0)
        second_part += jnp.sum(term.reshape(16, 16, 256), axis=0)
    second_part = summed(second_part, rows16)
    st_x[0] = jnp.concatenate(
        [
            jnp.concatenate([third_part[n * 8 : n * 8 + 8] for n in range(4)], axis=1),
            jnp.concatenate([second_part[0:8], second_part[8:16], jnp.zeros((8, 96), F32)], axis=1),
        ],
        axis=0,
    )
    copy(ST_X, st_x.at[0], st_x.at[1], {"seq_2": 1 - half})

    received(MIXED, first_in.at[pl.ds(0, N - 1)])
    mixed = nn(to_home, join_columns(mixed_in))
    out_ref[...] = (tok_ref[...].astype(F32) + mixed * activation).astype(BF)
    pre_grad = (upstream * mixed * sigmoid * (1.0 + gate * (1.0 - sigmoid))).astype(BF)
    pre_all[ch] = pre_grad
    to_ch(PRE, lambda peer: pre_all.at[ch], pre_all.at[ch])
    for p in range(4):
        gate_out[p * 32 : p * 32 + 32] = nn(tok_t[p], pre_grad).reshape(32, 8, 256).astype(BF)
    gate_in[me] = gate_out[me]
    to_seq(GATE, lambda peer: gate_out.at[peer], gate_in.at[me])

    received(ST_X, st_x.at[1])
    st_ch[ch] = st_x[0] + st_x[1]
    to_ch(ST_CH, lambda peer: st_ch.at[ch], st_ch.at[ch])

    received(BACK, grad_in.at[pl.ds(0, N - 1)])
    back_home = nn(to_home, join_columns(back_in)).astype(BF)
    parts, terms = [], []
    for b in range(4):
        rows = slice(b * 64, b * 64 + 64)
        parts.append(nt(back_home[rows], tok_ref[rows, :]))
        terms.append(tn(firsts[b], back_home[rows]))
    first_part = jnp.concatenate(
        [jnp.concatenate(parts[0:2], axis=0), jnp.concatenate(parts[2:4], axis=0)], axis=1
    )
    fg_out[...] = first_part.reshape(32, 4, 128)
    fg_in[row] = fg_out[row]

    def to_rows(d, carry):
        peer = lax.rem(row + d, 32)
        copy(FG_SUM, fg_out.at[peer], fg_in.at[row], place(peer * 4 + group))
        return carry

    lax.fori_loop(1, 32, to_rows, 0)

    received(ST_CH, st_ch.at[pl.ds(0, 3)])
    st_fin[...] = (st_ch[0] + st_ch[1] + st_ch[2] + st_ch[3]).astype(BF)
    st_ref[far] = st_fin[...]

    def to_columns(d, carry):
        peer = lax.rem(far + d, 64)
        copy(ST_ALL, st_fin, st_ref.at[far], place(peer * 2 + half))
        return carry

    lax.fori_loop(1, 64, to_columns, 0)

    received(PRE, pre_all.at[pl.ds(0, 3)])
    received(WROW, w_rows.at[pl.ds(0, 3)])
    back_gate = nt(pre_all[0], w_rows[0])
    for p in range(1, 4):
        back_gate += nt(pre_all[p], w_rows[p])
    ig_ref[...] = (upstream + jnp.concatenate(terms, axis=0) + back_gate).astype(BF)

    received(FG_SUM, fg_in.at[pl.ds(0, 31)])
    fg_ch[ch] = jnp.sum(fg_in[...], axis=0)
    to_ch(FG_CH, lambda peer: fg_ch.at[ch], fg_ch.at[ch])
    received(FG_CH, fg_ch.at[pl.ds(0, 3)])
    fg_fin[...] = (fg_ch[0] + fg_ch[1] + fg_ch[2] + fg_ch[3]).astype(BF)
    fg_ref[me] = fg_fin[...]
    to_seq(FG_ALL, lambda peer: fg_fin, fg_ref.at[me])

    received(GATE, gate_in.at[pl.ds(0, N - 1)])
    gg_ref[...] = jnp.sum(gate_in[...].astype(F32), axis=0)

    received(ST_ALL, st_ref.at[pl.ds(0, 63)])
    received(FG_ALL, fg_ref.at[pl.ds(0, N - 1)])

    for kind, part in (
        (TOK, tok_all.at[pl.ds(0, 3)]),
        (FIRST, first_in.at[pl.ds(0, N - 1)]),
        (WROW, w_rows.at[pl.ds(0, 3)]),
        (GRAD, grad_in.at[pl.ds(0, N - 1)]),
        (MIXED, first_in.at[pl.ds(0, N - 1)]),
        (BACK, first_in.at[pl.ds(0, N - 1)]),
        (PRE, pre_all.at[pl.ds(0, 3)]),
        (GATE, gate_in.at[pl.ds(0, N - 1)]),
        (FG_SUM, fg_in.at[pl.ds(0, 31)]),
        (FG_CH, fg_ch.at[pl.ds(0, 3)]),
        (FG_ALL, fg_ref.at[pl.ds(0, N - 1)]),
        (ST_X, st_x.at[0]),
        (ST_CH, st_ch.at[pl.ds(0, 3)]),
        (ST_ALL, st_ref.at[pl.ds(0, 63)]),
    ):
        sent(kind, part)


def on_device(tokens, cotangent, first_factor, second_factor, third_factor, gate_weight):
    whole = pl.BlockSpec(memory_space=pltpu.VMEM)
    vm = pltpu.VMEM
    output, input_grad, gate_grad, fg, st = pl.pallas_call(
        kernel,
        out_shape=(
            jax.ShapeDtypeStruct((256, 256), BF),
            jax.ShapeDtypeStruct((256, 256), BF),
            jax.ShapeDtypeStruct((8, 256), F32),
            jax.ShapeDtypeStruct((N, 4, 128), BF),
            jax.ShapeDtypeStruct((C, 16, 128), BF),
        ),
        in_specs=[whole] * 6,
        out_specs=[whole] * 5,
        scratch_shapes=[
            vm((4, 256, 256), BF),
            vm((4, 256, 256), BF),
            vm((4, 256, 256), BF),
            vm((4, 256, 256), BF),
            vm((2, C, 4, 128), BF),
            vm((N, 4, 128), BF),
            vm((2, C, 4, 128), BF),
            vm((N, 4, 128), BF),
            vm((N, 4, 128), BF),
            vm((2, C, 4, 128), BF),
            vm((N, 4, 128), BF),
            vm((2, C, 4, 128), BF),
            vm((512, 128), BF),
            vm((N, 8, 256), BF),
            vm((N, 8, 256), BF),
            vm((32, 4, 128), F32),
            vm((32, 4, 128), F32),
            vm((4, 4, 128), F32),
            vm((4, 128), BF),
            vm((2, 16, 128), F32),
            vm((4, 16, 128), F32),
            vm((16, 128), BF),
            pltpu.SemaphoreType.DMA((14,)),
            pltpu.SemaphoreType.DMA((14,)),
        ],
        compiler_params=pltpu.CompilerParams(
            collective_id=0, has_side_effects=True, vmem_limit_bytes=40 * 1024 * 1024
        ),
    )(tokens, cotangent, first_factor, second_factor, third_factor, gate_weight)
    first_grad = fg.reshape(2, 16, 4, 4, 2, 64).transpose(2, 4, 0, 1, 3, 5).reshape(B, C, C)
    third_grad = st[:, 0:8].reshape(C, 8, 4, 32).transpose(0, 2, 1, 3).reshape(C, A, A)
    second_grad = st[:, 8:16, 0:32].reshape(C, 8, 2, 16).transpose(0, 2, 1, 3).reshape(C, B, B)
    return output, input_grad, first_grad, second_grad, third_grad, gate_grad


def solution(mesh):
    torus = Mesh(mesh.devices.reshape(8, 8, 2, mesh.shape["ch"]), (*SEQ, "ch"))
    return jax.shard_map(
        on_device,
        mesh=torus,
        in_specs=(P(SEQ, "ch"), P(SEQ, "ch"), P(), P(), P(), P(None, "ch")),
        out_specs=(P(SEQ, "ch"), P(SEQ, "ch"), P(), P(), P(), P(SEQ, "ch")),
        check_vma=False,
    )
```

```python
import jax
import jax.numpy as jnp
from jax import lax
from jax.experimental import pallas as pl
from jax.experimental.pallas import tpu as pltpu
from jax.sharding import Mesh
from jax.sharding import PartitionSpec as P

A = 32
B = 16
C = 64
N = 128
SEQ = ("seq_0", "seq_1", "seq_2")
BF = jnp.bfloat16
F32 = jnp.float32
(
    TOK, TOK_FAR, TOK_LAST, FIRST, WROW, GRAD, MIXED, BACK, PRE, PRE_FAR, PRE_LAST,
    GATE_A, GATE_B, GATE_A2, GATE_B2, GATE_X, FG_SUM, FG_CH, FG_ALL, ST_X, ST_CH, ST_ALL,
) = range(22)


def place(s):
    return {"seq_0": s // 16, "seq_1": lax.rem(s // 2, 8), "seq_2": lax.rem(s, 2)}


def nn(x, y):
    return jnp.dot(x, y, preferred_element_type=F32)


def nt(x, y):
    return lax.dot_general(x, y, (((1,), (1,)), ((), ())), preferred_element_type=F32)


def tn(x, y):
    return lax.dot_general(x, y, (((0,), (0,)), ((), ())), preferred_element_type=F32)


def index(shape, dim):
    return lax.broadcasted_iota(jnp.int32, shape, dim)


def one_hot(flags):
    return jnp.where(flags, 1.0, 0.0).astype(BF)


def summed(x, ones):
    high = x.astype(BF)
    low = (x - high.astype(F32)).astype(BF)
    return nn(high, ones) + nn(low, ones)


def kernel(
    tok_hbm, cot_hbm, first_hbm, second_hbm, third_hbm, w_hbm,
    out_ref, ig_ref, gg_ref, fg_ref, st_ref,
    tok_ref, cot_ref, first_ref, second_ref, third_ref, w_ref,
    tok_all, tok_t, w_rows, pre_all,
    first_out, first_in, grad_out, grad_in, mixed_out, mixed_in, back_out, back_in,
    second_val, gate_a, gate_a_in, gate_b, gate_b_in, gate_a2, gate_a2_in, gate_b2, gate_b2_in,
    gate_x, gate_x_in, fg_out, fg_in, fg_ch, fg_fin, st_x, st_ch, st_fin,
    send_sem, recv_sem, load_sem, y_sem, x_sem,
):
    me = lax.axis_index(SEQ)
    ch = lax.axis_index("ch")
    far, half = me // 2, lax.rem(me, 2)
    row, group = me // 4, lax.rem(me, 4)
    at_z, at_y = me // 16, lax.rem(me // 2, 8)
    chip, core = ch // 2, lax.rem(ch, 2)
    sibling = chip * 2 + 1 - core
    across = (1 - chip) * 2 + core

    def copy(kind, src, dst, where):
        pltpu.make_async_remote_copy(
            src, dst, send_sem.at[kind], recv_sem.at[kind],
            device_id=where, device_id_type=pl.DeviceIdType.MESH,
        ).start()

    def greet(sem, where):
        pl.semaphore_signal(sem, inc=1, device_id=where, device_id_type=pl.DeviceIdType.MESH)

    def received(kind, part):
        pltpu.make_async_copy(part, part, recv_sem.at[kind]).wait()

    def sent(kind, part):
        pltpu.make_async_copy(part, part, send_sem.at[kind]).wait()

    def to_seq(kind, src, dst, first=1, last=N):
        def step(d, carry):
            peer = lax.rem(me + d, N)
            copy(kind, src(peer), dst, place(peer))
            return carry

        lax.fori_loop(first, last, step, 0)

    def to_ch(kind, src, dst):
        for d in (1, 2, 3):
            peer = lax.rem(ch + d, 4)
            copy(kind, src(peer), dst, {"ch": peer})

    def share(kind, buffer):
        copy(kind + 1, buffer.at[ch], buffer.at[ch], {"ch": across})
        copy(kind, buffer.at[ch], buffer.at[ch], {"ch": sibling})

    def pass_on(kind, buffer):
        received(kind + 1, buffer.at[across])
        copy(kind + 2, buffer.at[across], buffer.at[across], {"ch": sibling})

    barrier = pltpu.get_barrier_semaphore()
    for d in range(1, 8):
        greet(barrier, {"seq_0": lax.rem(at_z + d, 8)})
        greet(barrier, {"seq_1": lax.rem(at_y + d, 8)})
    greet(barrier, {"seq_2": 1 - half})
    for d in (1, 2, 3):
        greet(barrier, {"ch": lax.rem(ch + d, 4)})
    loads = [
        pltpu.make_async_copy(src, dst, load_sem.at[n])
        for n, (src, dst) in enumerate(
            (
                (tok_hbm, tok_ref), (first_hbm, first_ref), (second_hbm, second_ref),
                (third_hbm, third_ref), (cot_hbm, cot_ref), (w_hbm, w_ref),
            )
        )
    ]
    for load in loads:
        load.start()

    square = (256, 256)
    r, k = index(square, 0), index(square, 1)
    to_far = one_hot(k == (r & 3) * 64 + (r >> 2))
    to_home = one_hot(k == (r & 63) * 4 + (r >> 6))
    loads[0].wait()
    tok_all[ch] = nn(to_far, tok_ref[...]).astype(BF)
    loads[1].wait()
    spread_d = one_hot((index((64, 256), 1) & 63) == index((64, 256), 0))
    first_big = nn(jnp.concatenate([first_ref[group * 4 + b] for b in range(4)], axis=0), spread_d)
    first_big = jnp.where((r >> 6) == (k >> 6), first_big, 0.0).astype(BF)
    first_mat = nn(nn(to_far, first_big).astype(BF), to_home).astype(BF)
    first_back = nn(nt(to_far, first_big).astype(BF), to_home).astype(BF)

    def split_columns(values, buffer):
        for h in range(2):
            buffer[h] = values[:, h * 128 : h * 128 + 128].reshape(C, 4, 128)

    def join_columns(buffer):
        return jnp.concatenate([buffer[h].reshape(256, 128) for h in range(2)], axis=1)

    split_columns(nn(first_mat, tok_all[ch]).astype(BF), first_out)
    first_in[me] = first_out[half, far]

    rows32 = one_hot((index((512, 32), 0) >> 4) == index((512, 32), 1))
    rows16 = one_hot((index((256, 16), 0) & 15) == index((256, 16), 1))
    same_a = (r >> 4) == (k >> 4)
    same_b = (index((512, 512), 0) & 15) == (index((512, 512), 1) & 15)

    def own(ref, size):
        shape = (size, size, C)
        return jnp.sum(jnp.where(index(shape, 2) == far, ref[...].astype(F32), 0.0), axis=2).astype(BF)

    def spread_third(t):
        return jnp.where(same_b, nt(t.astype(BF), rows32), 0.0).astype(BF)

    def spread_second(t):
        return jnp.where(same_a, nt(t.astype(BF), rows16), 0.0).astype(BF)

    loads[2].wait()
    own_second = own(second_ref, B)
    second_mat = spread_second(nn(rows16, own_second))
    second_back = spread_second(nt(rows16, own_second))
    loads[3].wait()
    own_third = own(third_ref, A)
    third_mat, third_back = spread_third(nn(rows32, own_third)), spread_third(nt(rows32, own_third))
    loads[4].wait()
    upstream = nn(to_far, cot_ref[...])
    loads[5].wait()
    w_rows[ch] = w_ref[pl.ds(pl.multiple_of(ch * 256, 256), 256), :]

    def gate_term(p):
        return nn(tok_all[p], w_ref[pl.ds(pl.multiple_of(p * 256, 256), 256), :])

    gate = gate_term(ch)

    pl.semaphore_wait(barrier, 18)

    share(TOK, tok_all)
    for d in range(1, 8):
        greet(y_sem, {"seq_1": lax.rem(at_y + d, 8)})
    pl.semaphore_wait(y_sem, 7)
    greet(x_sem, {"seq_2": 1 - half})
    pl.semaphore_wait(x_sem, 1)

    def first_for(peer):
        return first_out.at[lax.rem(peer, 2), peer // 2]

    to_seq(FIRST, first_for, first_in.at[me], 1, 64)
    pass_on(TOK, tok_all)
    to_seq(FIRST, first_for, first_in.at[me], 64, N)

    received(TOK, tok_all.at[sibling])
    gate += gate_term(sibling) + gate_term(across)
    received(TOK_LAST, tok_all.at[0])
    gate += gate_term((1 - chip) * 2 + 1 - core)
    sigmoid = jax.nn.sigmoid(gate)
    activation = gate * sigmoid
    split_columns((upstream * activation).astype(BF), grad_out)
    grad_in[me] = grad_out[half, far]
    to_seq(GRAD, lambda peer: grad_out.at[lax.rem(peer, 2), peer // 2], grad_in.at[me])

    received(FIRST, first_in.at[pl.ds(0, N - 1)])
    far_first = first_in[...].reshape(512, 128)
    for h in range(2):
        second_val[h * 256 : h * 256 + 256, :] = nn(second_mat, far_first[h * 256 : h * 256 + 256]).astype(BF)
    mixed_out[...] = nn(third_mat, second_val[...]).astype(BF).reshape(N, 4, 128)
    mixed_in[half, far] = mixed_out[me]
    to_seq(MIXED, lambda peer: mixed_out.at[peer], mixed_in.at[half, far])
    to_ch(WROW, lambda peer: w_ref.at[pl.ds(pl.multiple_of(peer * 256, 256), 256), :], w_rows.at[ch])
    for p in range(4):
        tok_t[p] = tok_all[p].T

    received(GRAD, grad_in.at[pl.ds(0, N - 1)])
    far_grad = grad_in[...].reshape(512, 128)
    back_second = nn(third_back, far_grad).astype(BF)
    back_first = jnp.concatenate(
        [nn(second_back, back_second[h * 256 : h * 256 + 256]).astype(BF) for h in range(2)], axis=0
    )
    back_out[...] = back_first.reshape(N, 4, 128)
    back_in[half, far] = back_out[me]
    to_seq(BACK, lambda peer: back_out.at[peer], back_in.at[half, far])

    received(MIXED, first_in.at[pl.ds(0, N - 1)])
    mixed = join_columns(mixed_in).astype(F32)
    pre_grad = (upstream * mixed * sigmoid * (1.0 + gate * (1.0 - sigmoid))).astype(BF)
    pre_all[ch] = pre_grad
    share(PRE, pre_all)
    for p in range(4):
        term = nn(tok_t[p], pre_grad)
        gate_a[2 * p : 2 * p + 2] = term[:, 0:128].reshape(2, 128, 128).astype(BF)
        for n in range(16):
            gate_b[n % 8, 2 * p + n // 8] = term[n * 16 : n * 16 + 16, 128:256].astype(BF)
    gate_a_in[at_z] = gate_a[at_z]
    gate_b_in[at_y] = gate_b[at_y]
    for d in range(1, 8):
        peer_z, peer_y = lax.rem(at_z + d, 8), lax.rem(at_y + d, 8)
        copy(GATE_A, gate_a.at[peer_z], gate_a_in.at[at_z], {"seq_0": peer_z})
        copy(GATE_B, gate_b.at[peer_y], gate_b_in.at[at_y], {"seq_1": peer_y})

    third_part = jnp.where(same_b, nt(far_grad, second_val[...]), 0.0)
    third_part = summed(jnp.sum(third_part.reshape(A, B, 512), axis=1), rows32)
    second_part = jnp.zeros((16, 256), F32)
    for h in range(2):
        rows = slice(h * 256, h * 256 + 256)
        term = jnp.where(same_a, nt(back_second[rows], far_first[rows]), 0.0)
        second_part += jnp.sum(term.reshape(16, 16, 256), axis=0)
    second_part = summed(second_part, rows16)
    st_x[0] = jnp.concatenate(
        [
            jnp.concatenate([third_part[n * 8 : n * 8 + 8] for n in range(4)], axis=1),
            jnp.concatenate([second_part[0:8], second_part[8:16], jnp.zeros((8, 96), F32)], axis=1),
        ],
        axis=0,
    )
    copy(ST_X, st_x.at[0], st_x.at[1], {"seq_2": 1 - half})
    pass_on(PRE, pre_all)

    received(BACK, grad_in.at[pl.ds(0, N - 1)])
    back_home = join_columns(back_in)
    first_part = jnp.where((r & 3) == (k & 3), nt(back_home, tok_all[ch]), 0.0)
    first_part = summed(first_part, one_hot((index((256, 64), 0) >> 2) == index((256, 64), 1)))
    fg_out[...] = jnp.concatenate([first_part[0:128], first_part[128:256]], axis=1).reshape(32, 4, 128)
    fg_in[row] = fg_out[row]

    def to_rows(d, carry):
        peer = lax.rem(row + d, 32)
        copy(FG_SUM, fg_out.at[peer], fg_in.at[row], place(peer * 4 + group))
        return carry

    lax.fori_loop(1, 32, to_rows, 0)

    received(ST_X, st_x.at[1])
    st_ch[ch] = st_x[0] + st_x[1]
    to_ch(ST_CH, lambda peer: st_ch.at[ch], st_ch.at[ch])

    received(GATE_A, gate_a_in.at[pl.ds(0, 7)])
    gate_a2[...] = jnp.sum(gate_a_in[...].astype(F32), axis=0).astype(BF).reshape(8, 16, 128)
    received(GATE_B, gate_b_in.at[pl.ds(0, 7)])
    gate_b2[...] = jnp.sum(gate_b_in[...].astype(F32), axis=0).astype(BF)
    gate_a2_in[at_y] = gate_a2[at_y]
    gate_b2_in[at_z] = gate_b2[at_z]
    for d in range(1, 8):
        peer_z, peer_y = lax.rem(at_z + d, 8), lax.rem(at_y + d, 8)
        copy(GATE_A2, gate_a2.at[peer_y], gate_a2_in.at[at_y], {"seq_1": peer_y})
        copy(GATE_B2, gate_b2.at[peer_z], gate_b2_in.at[at_z], {"seq_0": peer_z})

    received(FG_SUM, fg_in.at[pl.ds(0, 31)])
    fg_ch[ch] = jnp.sum(fg_in[...], axis=0)
    to_ch(FG_CH, lambda peer: fg_ch.at[ch], fg_ch.at[ch])

    received(ST_CH, st_ch.at[pl.ds(0, 3)])
    st_fin[...] = (st_ch[0] + st_ch[1] + st_ch[2] + st_ch[3]).astype(BF)
    st_ref[far] = st_fin[...]

    def to_columns(d, carry):
        peer = lax.rem(far + d, 64)
        copy(ST_ALL, st_fin, st_ref.at[far], place(peer * 2 + half))
        return carry

    lax.fori_loop(1, 64, to_columns, 0)

    received(FG_CH, fg_ch.at[pl.ds(0, 3)])
    fg_fin[...] = (fg_ch[0] + fg_ch[1] + fg_ch[2] + fg_ch[3]).astype(BF)
    fg_ref[me] = fg_fin[...]
    to_seq(FG_ALL, lambda peer: fg_fin, fg_ref.at[me])

    received(GATE_A2, gate_a2_in.at[pl.ds(0, 7)])
    received(GATE_B2, gate_b2_in.at[pl.ds(0, 7)])
    gate_sum = jnp.concatenate(
        [jnp.sum(part[...].astype(F32), axis=0) for part in (gate_a2_in, gate_b2_in)], axis=1
    )
    gate_x[0] = gate_sum[0:8]
    gate_x[1] = gate_sum[8:16]
    copy(GATE_X, gate_x.at[1 - half], gate_x_in, {"seq_2": 1 - half})

    out_ref[...] = nn(to_home, (tok_all[ch].astype(F32) + mixed * activation).astype(BF)).astype(BF)
    received(PRE, pre_all.at[0])
    received(PRE_LAST, pre_all.at[0])
    received(WROW, w_rows.at[pl.ds(0, 3)])
    in_grad = upstream + nn(first_back, back_home)
    for p in range(4):
        in_grad += nt(pre_all[p], w_rows[p])
    ig_ref[...] = nn(to_home, in_grad.astype(BF)).astype(BF)
    received(GATE_X, gate_x_in)
    gg_ref[...] = gate_x[half] + gate_x_in[...]

    received(ST_ALL, st_ref.at[pl.ds(0, 63)])
    received(FG_ALL, fg_ref.at[pl.ds(0, N - 1)])

    for kind, part in (
        (TOK, tok_all.at[0]),
        (TOK_FAR, tok_all.at[0]),
        (TOK_LAST, tok_all.at[0]),
        (FIRST, first_in.at[pl.ds(0, N - 1)]),
        (WROW, w_rows.at[pl.ds(0, 3)]),
        (GRAD, grad_in.at[pl.ds(0, N - 1)]),
        (MIXED, first_in.at[pl.ds(0, N - 1)]),
        (BACK, first_in.at[pl.ds(0, N - 1)]),
        (PRE, pre_all.at[0]),
        (PRE_FAR, pre_all.at[0]),
        (PRE_LAST, pre_all.at[0]),
        (GATE_A, gate_a_in.at[pl.ds(0, 7)]),
        (GATE_B, gate_b_in.at[pl.ds(0, 7)]),
        (GATE_A2, gate_a2_in.at[pl.ds(0, 7)]),
        (GATE_B2, gate_b2_in.at[pl.ds(0, 7)]),
        (GATE_X, gate_x_in),
        (FG_SUM, fg_in.at[pl.ds(0, 31)]),
        (FG_CH, fg_ch.at[pl.ds(0, 3)]),
        (FG_ALL, fg_ref.at[pl.ds(0, N - 1)]),
        (ST_X, st_x.at[0]),
        (ST_CH, st_ch.at[pl.ds(0, 3)]),
        (ST_ALL, st_ref.at[pl.ds(0, 63)]),
    ):
        sent(kind, part)


def on_device(tokens, cotangent, first_factor, second_factor, third_factor, gate_weight):
    whole = pl.BlockSpec(memory_space=pltpu.VMEM)
    vm = pltpu.VMEM
    output, input_grad, gate_grad, fg, st = pl.pallas_call(
        kernel,
        out_shape=(
            jax.ShapeDtypeStruct((256, 256), BF),
            jax.ShapeDtypeStruct((256, 256), BF),
            jax.ShapeDtypeStruct((8, 256), F32),
            jax.ShapeDtypeStruct((N, 4, 128), BF),
            jax.ShapeDtypeStruct((C, 16, 128), BF),
        ),
        in_specs=[pl.BlockSpec(memory_space=pl.ANY)] * 6,
        out_specs=[whole] * 5,
        scratch_shapes=[
            vm((256, 256), BF),
            vm((256, 256), BF),
            vm((B, C, C), BF),
            vm((B, B, C), BF),
            vm((A, A, C), BF),
            vm((1024, 256), BF),
            *[vm((4, 256, 256), BF)] * 4,
            vm((2, C, 4, 128), BF),
            vm((N, 4, 128), BF),
            vm((2, C, 4, 128), BF),
            vm((N, 4, 128), BF),
            vm((N, 4, 128), BF),
            vm((2, C, 4, 128), BF),
            vm((N, 4, 128), BF),
            vm((2, C, 4, 128), BF),
            vm((512, 128), BF),
            *[vm((8, 128, 128), BF)] * 2,
            *[vm((8, 8, 16, 128), BF)] * 2,
            *[vm((8, 16, 128), BF)] * 4,
            vm((2, 8, 256), F32),
            vm((8, 256), F32),
            vm((32, 4, 128), F32),
            vm((32, 4, 128), F32),
            vm((4, 4, 128), F32),
            vm((4, 128), BF),
            vm((2, 16, 128), F32),
            vm((4, 16, 128), F32),
            vm((16, 128), BF),
            pltpu.SemaphoreType.DMA((22,)),
            pltpu.SemaphoreType.DMA((22,)),
            pltpu.SemaphoreType.DMA((6,)),
            pltpu.SemaphoreType.REGULAR,
            pltpu.SemaphoreType.REGULAR,
        ],
        compiler_params=pltpu.CompilerParams(
            collective_id=0, has_side_effects=True, vmem_limit_bytes=56 * 1024 * 1024
        ),
    )(
        tokens,
        cotangent,
        first_factor,
        second_factor.transpose(1, 2, 0),
        third_factor.transpose(1, 2, 0),
        gate_weight,
    )
    first_grad = fg.reshape(32, 4, 4, 2, 64).transpose(1, 2, 3, 0, 4).reshape(B, C, C)
    third_grad = st[:, 0:8].reshape(C, 8, 4, 32).transpose(0, 2, 1, 3).reshape(C, A, A)
    second_grad = st[:, 8:16, 0:32].reshape(C, 8, 2, 16).transpose(0, 2, 1, 3).reshape(C, B, B)
    return output, input_grad, first_grad, second_grad, third_grad, gate_grad


def solution(mesh):
    torus = Mesh(mesh.devices.reshape(8, 8, 2, mesh.shape["ch"]), (*SEQ, "ch"))
    return jax.shard_map(
        on_device,
        mesh=torus,
        in_specs=(P(SEQ, "ch"), P(SEQ, "ch"), P(), P(), P(), P(None, "ch")),
        out_specs=(P(SEQ, "ch"), P(SEQ, "ch"), P(), P(), P(), P(SEQ, "ch")),
        check_vma=False,
    )
```

```python
import jax
import jax.numpy as jnp
from jax import lax
from jax.experimental import pallas as pl
from jax.experimental.pallas import tpu as pltpu
from jax.sharding import Mesh
from jax.sharding import PartitionSpec as P

A = 32
B = 16
C = 64
N = 128
SEQ = ("seq_0", "seq_1", "seq_2")
BF = jnp.bfloat16
F32 = jnp.float32
(
    TOK, TOK_FAR, TOK_LAST, FIRST, GRAD, MIXED, BACK, PAIR, ACROSS,
    GATE_A, GATE_B, GATE_A2, GATE_B2, GATE_X, FG_SUM, FG_CH, FG_ALL, ST_X, ST_CH, ST_ALL,
) = range(20)


def place(s):
    return {"seq_0": s // 16, "seq_1": lax.rem(s // 2, 8), "seq_2": lax.rem(s, 2)}


def nn(x, y):
    return jnp.dot(x, y, preferred_element_type=F32)


def nt(x, y):
    return lax.dot_general(x, y, (((1,), (1,)), ((), ())), preferred_element_type=F32)


def tn(x, y):
    return lax.dot_general(x, y, (((0,), (0,)), ((), ())), preferred_element_type=F32)


def index(shape, dim):
    return lax.broadcasted_iota(jnp.int32, shape, dim)


def one_hot(flags):
    return jnp.where(flags, 1.0, 0.0).astype(BF)


def summed(x, ones):
    high = x.astype(BF)
    low = (x - high.astype(F32)).astype(BF)
    return nn(high, ones) + nn(low, ones)


def kernel(
    tok_hbm, cot_hbm, first_hbm, second_hbm, third_hbm, w_hbm,
    out_hbm, ig_hbm, gg_hbm, first_hbm_grad, second_hbm_grad, third_hbm_grad,
    out_ref, ig_ref, gg_ref, first_grad, second_grad, third_grad,
    tok_ref, cot_ref, first_ref, second_ref, third_ref, w_ref,
    tok_all, tok_t, pair_out, pair_in, across_out, across_in, input_part,
    first_out, first_in, grad_out, grad_in, mixed_out, mixed_in, back_out, back_in,
    second_val, gate_a, gate_a_in, gate_b, gate_b_in, gate_a2, gate_a2_in, gate_b2, gate_b2_in,
    gate_x, gate_x_in, fg_out, fg_in, fg_ch, fg_fin, fg_ref, st_x, st_ch, st_fin, st_ref, st_rows,
    send_sem, recv_sem, load_sem, store_sem, y_sem, x_sem,
):
    me = lax.axis_index(SEQ)
    ch = lax.axis_index("ch")
    far, half = me // 2, lax.rem(me, 2)
    row, group = me // 4, lax.rem(me, 4)
    at_z, at_y = me // 16, lax.rem(me // 2, 8)
    chip, core = ch // 2, lax.rem(ch, 2)
    sibling = chip * 2 + 1 - core
    across = (1 - chip) * 2 + core
    corner = (1 - chip) * 2 + 1 - core

    def copy(kind, src, dst, where):
        pltpu.make_async_remote_copy(
            src, dst, send_sem.at[kind], recv_sem.at[kind],
            device_id=where, device_id_type=pl.DeviceIdType.MESH,
        ).start()

    def greet(sem, where):
        pl.semaphore_signal(sem, inc=1, device_id=where, device_id_type=pl.DeviceIdType.MESH)

    def received(kind, part):
        pltpu.make_async_copy(part, part, recv_sem.at[kind]).wait()

    def sent(kind, part):
        pltpu.make_async_copy(part, part, send_sem.at[kind]).wait()

    def to_seq(kind, src, dst, first=1, last=N):
        def step(d, carry):
            peer = lax.rem(me + d, N)
            copy(kind, src(peer), dst, place(peer))
            return carry

        lax.fori_loop(first, last, step, 0)

    def to_ch(kind, src, dst):
        for d in (1, 2, 3):
            peer = lax.rem(ch + d, 4)
            copy(kind, src(peer), dst, {"ch": peer})

    def share(kind, buffer):
        copy(kind + 1, buffer.at[ch], buffer.at[ch], {"ch": across})
        copy(kind, buffer.at[ch], buffer.at[ch], {"ch": sibling})

    def pass_on(kind, buffer):
        received(kind + 1, buffer.at[across])
        copy(kind + 2, buffer.at[across], buffer.at[across], {"ch": sibling})

    barrier = pltpu.get_barrier_semaphore()
    for d in range(1, 8):
        greet(barrier, {"seq_0": lax.rem(at_z + d, 8)})
        greet(barrier, {"seq_1": lax.rem(at_y + d, 8)})
    greet(barrier, {"seq_2": 1 - half})
    for d in (1, 2, 3):
        greet(barrier, {"ch": lax.rem(ch + d, 4)})
    loads = [
        pltpu.make_async_copy(src, dst, load_sem.at[n])
        for n, (src, dst) in enumerate(
            (
                (tok_hbm, tok_ref), (first_hbm, first_ref), (second_hbm, second_ref),
                (third_hbm, third_ref), (cot_hbm, cot_ref), (w_hbm, w_ref),
            )
        )
    ]
    for load in loads:
        load.start()
    stores = [
        pltpu.make_async_copy(src, dst, store_sem.at[n])
        for n, (src, dst) in enumerate(
            (
                (out_ref, out_hbm), (ig_ref, ig_hbm), (gg_ref, gg_hbm),
                (first_grad, first_hbm_grad), (second_grad, second_hbm_grad), (third_grad, third_hbm_grad),
            )
        )
    ]

    square = (256, 256)
    r, k = index(square, 0), index(square, 1)
    to_far = one_hot(k == (r & 3) * 64 + (r >> 2))
    to_home = one_hot(k == (r & 63) * 4 + (r >> 6))
    loads[0].wait()
    tok_all[ch] = nn(to_far, tok_ref[...]).astype(BF)
    loads[1].wait()
    spread_d = one_hot((index((64, 256), 1) & 63) == index((64, 256), 0))
    first_big = nn(jnp.concatenate([first_ref[group * 4 + b] for b in range(4)], axis=0), spread_d)
    first_big = jnp.where((r >> 6) == (k >> 6), first_big, 0.0).astype(BF)
    first_mat = nn(nn(to_far, first_big).astype(BF), to_home).astype(BF)
    first_back = nn(nt(to_far, first_big).astype(BF), to_home).astype(BF)

    def split_columns(values, buffer):
        for h in range(2):
            buffer[h] = values[:, h * 128 : h * 128 + 128].reshape(C, 4, 128)

    def join_columns(buffer):
        return jnp.concatenate([buffer[h].reshape(256, 128) for h in range(2)], axis=1)

    split_columns(nn(first_mat, tok_all[ch]).astype(BF), first_out)
    first_in[me] = first_out[half, far]

    rows32 = one_hot((index((512, 32), 0) >> 4) == index((512, 32), 1))
    rows16 = one_hot((index((256, 16), 0) & 15) == index((256, 16), 1))
    same_a = (r >> 4) == (k >> 4)
    same_b = (index((512, 512), 0) & 15) == (index((512, 512), 1) & 15)

    def own(ref, size):
        shape = (size, size, C)
        return jnp.sum(jnp.where(index(shape, 2) == far, ref[...].astype(F32), 0.0), axis=2).astype(BF)

    def spread_third(t):
        return jnp.where(same_b, nt(t.astype(BF), rows32), 0.0).astype(BF)

    def spread_second(t):
        return jnp.where(same_a, nt(t.astype(BF), rows16), 0.0).astype(BF)

    loads[2].wait()
    own_second = own(second_ref, B)
    second_mat = spread_second(nn(rows16, own_second))
    second_back = spread_second(nt(rows16, own_second))
    loads[3].wait()
    own_third = own(third_ref, A)
    third_mat, third_back = spread_third(nn(rows32, own_third)), spread_third(nt(rows32, own_third))
    loads[4].wait()
    upstream = nn(to_far, cot_ref[...])
    loads[5].wait()

    def w_rows(p):
        return w_ref[pl.ds(pl.multiple_of(p * 256, 256), 256), :]

    def gate_term(p):
        return nn(tok_all[p], w_rows(p))

    gate = gate_term(ch)

    pl.semaphore_wait(barrier, 18)

    share(TOK, tok_all)
    for d in range(1, 8):
        greet(y_sem, {"seq_1": lax.rem(at_y + d, 8)})
    pl.semaphore_wait(y_sem, 7)
    greet(x_sem, {"seq_2": 1 - half})
    pl.semaphore_wait(x_sem, 1)

    def first_for(peer):
        return first_out.at[lax.rem(peer, 2), peer // 2]

    to_seq(FIRST, first_for, first_in.at[me], 1, 64)
    pass_on(TOK, tok_all)
    to_seq(FIRST, first_for, first_in.at[me], 64, N)

    received(TOK, tok_all.at[sibling])
    gate += gate_term(sibling) + gate_term(across)
    received(TOK_LAST, tok_all.at[0])
    gate += gate_term(corner)
    sigmoid = jax.nn.sigmoid(gate)
    activation = gate * sigmoid
    split_columns((upstream * activation).astype(BF), grad_out)
    grad_in[me] = grad_out[half, far]
    to_seq(GRAD, lambda peer: grad_out.at[lax.rem(peer, 2), peer // 2], grad_in.at[me])

    received(FIRST, first_in.at[pl.ds(0, N - 1)])
    far_first = first_in[...].reshape(512, 128)
    for h in range(2):
        second_val[h * 256 : h * 256 + 256, :] = nn(second_mat, far_first[h * 256 : h * 256 + 256]).astype(BF)
    mixed_out[...] = nn(third_mat, second_val[...]).astype(BF).reshape(N, 4, 128)
    mixed_in[half, far] = mixed_out[me]
    to_seq(MIXED, lambda peer: mixed_out.at[peer], mixed_in.at[half, far])
    for p in range(4):
        tok_t[p] = tok_all[p].T

    received(GRAD, grad_in.at[pl.ds(0, N - 1)])
    far_grad = grad_in[...].reshape(512, 128)
    back_second = nn(third_back, far_grad).astype(BF)
    back_first = jnp.concatenate(
        [nn(second_back, back_second[h * 256 : h * 256 + 256]).astype(BF) for h in range(2)], axis=0
    )
    back_out[...] = back_first.reshape(N, 4, 128)
    back_in[half, far] = back_out[me]
    to_seq(BACK, lambda peer: back_out.at[peer], back_in.at[half, far])

    received(MIXED, first_in.at[pl.ds(0, N - 1)])
    mixed = join_columns(mixed_in).astype(F32)
    pre_grad = (upstream * mixed * sigmoid * (1.0 + gate * (1.0 - sigmoid))).astype(BF)
    for p in range(4):
        term = nn(tok_t[p], pre_grad)
        gate_a[2 * p : 2 * p + 2] = term[:, 0:128].reshape(2, 128, 128).astype(BF)
        for n in range(16):
            gate_b[n % 8, 2 * p + n // 8] = term[n * 16 : n * 16 + 16, 128:256].astype(BF)
    gate_a_in[at_z] = gate_a[at_z]
    gate_b_in[at_y] = gate_b[at_y]
    for d in range(1, 8):
        peer_z, peer_y = lax.rem(at_z + d, 8), lax.rem(at_y + d, 8)
        copy(GATE_A, gate_a.at[peer_z], gate_a_in.at[at_z], {"seq_0": peer_z})
        copy(GATE_B, gate_b.at[peer_y], gate_b_in.at[at_y], {"seq_1": peer_y})

    pair_out[0] = nt(pre_grad, w_rows(sibling)).astype(BF)
    pair_out[1] = nt(pre_grad, w_rows(corner)).astype(BF)
    copy(PAIR, pair_out, pair_in, {"ch": sibling})
    input_part[0] = nt(pre_grad, w_rows(ch))
    input_part[1] = nt(pre_grad, w_rows(across))

    third_part = jnp.where(same_b, nt(far_grad, second_val[...]), 0.0)
    third_part = summed(jnp.sum(third_part.reshape(A, B, 512), axis=1), rows32)
    second_part = jnp.zeros((16, 256), F32)
    for h in range(2):
        rows = slice(h * 256, h * 256 + 256)
        term = jnp.where(same_a, nt(back_second[rows], far_first[rows]), 0.0)
        second_part += jnp.sum(term.reshape(16, 16, 256), axis=0)
    second_part = summed(second_part, rows16)
    st_x[0] = jnp.concatenate(
        [
            jnp.concatenate([third_part[n * 8 : n * 8 + 8] for n in range(4)], axis=1),
            jnp.concatenate([second_part[0:8], second_part[8:16], jnp.zeros((8, 96), F32)], axis=1),
        ],
        axis=0,
    )
    copy(ST_X, st_x.at[0], st_x.at[1], {"seq_2": 1 - half})
    received(PAIR, pair_in)
    across_out[...] = (input_part[1] + pair_in[1].astype(F32)).astype(BF)
    copy(ACROSS, across_out, across_in, {"ch": across})

    received(BACK, grad_in.at[pl.ds(0, N - 1)])
    back_home = join_columns(back_in)
    first_part = jnp.where((r & 3) == (k & 3), nt(back_home, tok_all[ch]), 0.0)
    first_part = summed(first_part, one_hot((index((256, 64), 0) >> 2) == index((256, 64), 1)))
    fg_out[...] = jnp.concatenate([first_part[0:128], first_part[128:256]], axis=1).reshape(32, 4, 128)
    fg_in[row] = fg_out[row]

    def to_rows(d, carry):
        peer = lax.rem(row + d, 32)
        copy(FG_SUM, fg_out.at[peer], fg_in.at[row], place(peer * 4 + group))
        return carry

    lax.fori_loop(1, 32, to_rows, 0)

    received(ST_X, st_x.at[1])
    st_ch[ch] = st_x[0] + st_x[1]
    to_ch(ST_CH, lambda peer: st_ch.at[ch], st_ch.at[ch])

    received(GATE_A, gate_a_in.at[pl.ds(0, 7)])
    gate_a2[...] = jnp.sum(gate_a_in[...].astype(F32), axis=0).astype(BF).reshape(8, 16, 128)
    received(GATE_B, gate_b_in.at[pl.ds(0, 7)])
    gate_b2[...] = jnp.sum(gate_b_in[...].astype(F32), axis=0).astype(BF)
    gate_a2_in[at_y] = gate_a2[at_y]
    gate_b2_in[at_z] = gate_b2[at_z]
    for d in range(1, 8):
        peer_z, peer_y = lax.rem(at_z + d, 8), lax.rem(at_y + d, 8)
        copy(GATE_A2, gate_a2.at[peer_y], gate_a2_in.at[at_y], {"seq_1": peer_y})
        copy(GATE_B2, gate_b2.at[peer_z], gate_b2_in.at[at_z], {"seq_0": peer_z})

    received(FG_SUM, fg_in.at[pl.ds(0, 31)])
    fg_ch[ch] = jnp.sum(fg_in[...], axis=0)
    to_ch(FG_CH, lambda peer: fg_ch.at[ch], fg_ch.at[ch])

    received(ST_CH, st_ch.at[pl.ds(0, 3)])
    st_fin[...] = (st_ch[0] + st_ch[1] + st_ch[2] + st_ch[3]).astype(BF)
    st_ref[far] = st_fin[...]

    def to_columns(d, carry):
        peer = lax.rem(far + d, 64)
        copy(ST_ALL, st_fin, st_ref.at[far], place(peer * 2 + half))
        return carry

    lax.fori_loop(1, 64, to_columns, 0)

    received(FG_CH, fg_ch.at[pl.ds(0, 3)])
    fg_fin[...] = (fg_ch[0] + fg_ch[1] + fg_ch[2] + fg_ch[3]).astype(BF)
    fg_ref[me] = fg_fin[...]
    to_seq(FG_ALL, lambda peer: fg_fin, fg_ref.at[me])

    received(GATE_A2, gate_a2_in.at[pl.ds(0, 7)])
    received(GATE_B2, gate_b2_in.at[pl.ds(0, 7)])
    gate_sum = jnp.concatenate(
        [jnp.sum(part[...].astype(F32), axis=0) for part in (gate_a2_in, gate_b2_in)], axis=1
    )
    gate_x[0] = gate_sum[0:8]
    gate_x[1] = gate_sum[8:16]
    copy(GATE_X, gate_x.at[1 - half], gate_x_in, {"seq_2": 1 - half})

    out_ref[...] = nn(to_home, (tok_all[ch].astype(F32) + mixed * activation).astype(BF)).astype(BF)
    stores[0].start()
    received(ACROSS, across_in)
    in_grad = upstream + nn(first_back, back_home) + input_part[0]
    in_grad += pair_in[0].astype(F32) + across_in[...].astype(F32)
    ig_ref[...] = nn(to_home, in_grad.astype(BF)).astype(BF)
    stores[1].start()
    received(GATE_X, gate_x_in)
    gg_ref[...] = gate_x[half] + gate_x_in[...]
    stores[2].start()

    by_part = one_hot(k == (r & 15) * 16 + (r >> 4))
    by_block = one_hot(
        index((512, 512), 1) == (index((512, 512), 0) & 31) * 16 + (index((512, 512), 0) >> 5)
    )
    eye = one_hot(index((128, 128), 0) == index((128, 128), 1))
    received(ST_ALL, st_ref.at[pl.ds(0, 63)])
    for g in range(4):
        block = st_ref[g * 16 : g * 16 + 16].reshape(256, 128)
        st_rows[:, g * 16 : g * 16 + 16, :] = nn(by_part, block).astype(BF).reshape(16, 16, 128)
    for n in range(8):
        turned = nt(eye, st_rows[n]).astype(BF)
        for m in range(4):
            third_grad[m * 8 + n] = turned[m * 32 : m * 32 + 32]
    stores[5].start()
    for n in range(8):
        turned = nt(eye[0:32], st_rows[8 + n]).astype(BF)
        for m in range(2):
            second_grad[m * 8 + n] = turned[m * 16 : m * 16 + 16]
    stores[4].start()
    received(FG_ALL, fg_ref.at[pl.ds(0, N - 1)])
    blocks = nn(by_block, fg_ref[...].reshape(512, 128)).astype(BF).reshape(B, 32, 128)
    for h in range(2):
        first_grad[:, h * 32 : h * 32 + 32, :] = blocks[:, :, h * 64 : h * 64 + 64]
    stores[3].start()

    for kind, part in (
        (TOK, tok_all.at[0]),
        (TOK_FAR, tok_all.at[0]),
        (TOK_LAST, tok_all.at[0]),
        (FIRST, first_in.at[pl.ds(0, N - 1)]),
        (GRAD, grad_in.at[pl.ds(0, N - 1)]),
        (MIXED, first_in.at[pl.ds(0, N - 1)]),
        (BACK, first_in.at[pl.ds(0, N - 1)]),
        (PAIR, pair_out),
        (ACROSS, across_out),
        (GATE_A, gate_a_in.at[pl.ds(0, 7)]),
        (GATE_B, gate_b_in.at[pl.ds(0, 7)]),
        (GATE_A2, gate_a2_in.at[pl.ds(0, 7)]),
        (GATE_B2, gate_b2_in.at[pl.ds(0, 7)]),
        (GATE_X, gate_x_in),
        (FG_SUM, fg_in.at[pl.ds(0, 31)]),
        (FG_CH, fg_ch.at[pl.ds(0, 3)]),
        (FG_ALL, fg_ref.at[pl.ds(0, N - 1)]),
        (ST_X, st_x.at[0]),
        (ST_CH, st_ch.at[pl.ds(0, 3)]),
        (ST_ALL, st_ref.at[pl.ds(0, 63)]),
    ):
        sent(kind, part)
    for store in stores:
        store.wait()


def copies(*refs):
    sources, results, held = refs[0:6], refs[6:12], refs[12:18]
    load_sem, store_sem = refs[18:20]
    loads = [pltpu.make_async_copy(sources[n], held[n], load_sem.at[n]) for n in range(6)]
    stores = [pltpu.make_async_copy(held[n], results[n], store_sem.at[n]) for n in range(6)]
    for load in loads:
        load.start()
    for load, store in zip(loads, stores):
        load.wait()
        store.start()
    for store in stores:
        store.wait()


def on_device(tokens, cotangent, first_factor, second_factor, third_factor, gate_weight):
    vm = pltpu.VMEM
    anywhere = pl.BlockSpec(memory_space=pl.ANY)
    shapes = (
        jax.ShapeDtypeStruct((256, 256), BF),
        jax.ShapeDtypeStruct((256, 256), BF),
        jax.ShapeDtypeStruct((8, 256), F32),
        jax.ShapeDtypeStruct((B, C, C), BF),
        jax.ShapeDtypeStruct((B, B, C), BF),
        jax.ShapeDtypeStruct((A, A, C), BF),
    )
    results = pl.pallas_call(
        kernel,
        out_shape=shapes,
        in_specs=[anywhere] * 6,
        out_specs=[anywhere] * 6,
        scratch_shapes=[
            *[vm(shape.shape, shape.dtype) for shape in shapes],
            vm((256, 256), BF),
            vm((256, 256), BF),
            vm((B, C, C), BF),
            vm((B, B, C), BF),
            vm((A, A, C), BF),
            vm((1024, 256), BF),
            *[vm((4, 256, 256), BF)] * 2,
            *[vm((2, 256, 256), BF)] * 2,
            *[vm((256, 256), BF)] * 2,
            vm((2, 256, 256), F32),
            vm((2, C, 4, 128), BF),
            vm((N, 4, 128), BF),
            vm((2, C, 4, 128), BF),
            vm((N, 4, 128), BF),
            vm((N, 4, 128), BF),
            vm((2, C, 4, 128), BF),
            vm((N, 4, 128), BF),
            vm((2, C, 4, 128), BF),
            vm((512, 128), BF),
            *[vm((8, 128, 128), BF)] * 2,
            *[vm((8, 8, 16, 128), BF)] * 2,
            *[vm((8, 16, 128), BF)] * 4,
            vm((2, 8, 256), F32),
            vm((8, 256), F32),
            vm((32, 4, 128), F32),
            vm((32, 4, 128), F32),
            vm((4, 4, 128), F32),
            vm((4, 128), BF),
            vm((N, 4, 128), BF),
            vm((2, 16, 128), F32),
            vm((4, 16, 128), F32),
            vm((16, 128), BF),
            vm((C, 16, 128), BF),
            vm((16, C, 128), BF),
            pltpu.SemaphoreType.DMA((20,)),
            pltpu.SemaphoreType.DMA((20,)),
            pltpu.SemaphoreType.DMA((6,)),
            pltpu.SemaphoreType.DMA((6,)),
            pltpu.SemaphoreType.REGULAR,
            pltpu.SemaphoreType.REGULAR,
        ],
        compiler_params=pltpu.CompilerParams(
            collective_id=0, has_side_effects=True, vmem_limit_bytes=56 * 1024 * 1024
        ),
    )(
        tokens,
        cotangent,
        first_factor,
        second_factor.transpose(1, 2, 0),
        third_factor.transpose(1, 2, 0),
        gate_weight,
    )
    output, input_grad, gate_grad, first, second, third = pl.pallas_call(
        copies,
        out_shape=shapes,
        in_specs=[anywhere] * 6,
        out_specs=[anywhere] * 6,
        scratch_shapes=[
            *[vm(shape.shape, shape.dtype) for shape in shapes],
            pltpu.SemaphoreType.DMA((6,)),
            pltpu.SemaphoreType.DMA((6,)),
        ],
    )(*results)
    return output, input_grad, first, second.transpose(2, 0, 1), third.transpose(2, 0, 1), gate_grad


def solution(mesh):
    torus = Mesh(mesh.devices.reshape(8, 8, 2, mesh.shape["ch"]), (*SEQ, "ch"))
    return jax.shard_map(
        on_device,
        mesh=torus,
        in_specs=(P(SEQ, "ch"), P(SEQ, "ch"), P(), P(), P(), P(None, "ch")),
        out_specs=(P(SEQ, "ch"), P(SEQ, "ch"), P(), P(), P(), P(SEQ, "ch")),
        check_vma=False,
    )
```

```python
import jax
import jax.numpy as jnp
from jax import lax
from jax.experimental import pallas as pl
from jax.experimental.pallas import tpu as pltpu
from jax.sharding import Mesh
from jax.sharding import PartitionSpec as P

A = 32
B = 16
C = 64
N = 128
SEQ = ("seq_0", "seq_1", "seq_2")
BF = jnp.bfloat16
F32 = jnp.float32
(
    TOK, TOK_FAR, TOK_LAST, FIRST, GRAD, MIXED, BACK, PAIR, ACROSS,
    GATE_A, GATE_B, GATE_A2, GATE_B2, GATE_X, FG_SUM, FG_CH, FG_ALL, ST_X, ST_CH, ST_ALL,
) = range(20)


def place(s):
    return {"seq_0": s // 16, "seq_1": lax.rem(s // 2, 8), "seq_2": lax.rem(s, 2)}


def nn(x, y):
    return jnp.dot(x, y, preferred_element_type=F32)


def nt(x, y):
    return lax.dot_general(x, y, (((1,), (1,)), ((), ())), preferred_element_type=F32)


def tn(x, y):
    return lax.dot_general(x, y, (((0,), (0,)), ((), ())), preferred_element_type=F32)


def index(shape, dim):
    return lax.broadcasted_iota(jnp.int32, shape, dim)


def one_hot(flags):
    return jnp.where(flags, 1.0, 0.0).astype(BF)


def summed(x, ones):
    high = x.astype(BF)
    low = (x - high.astype(F32)).astype(BF)
    return nn(high, ones) + nn(low, ones)


def kernel(
    tok_hbm, cot_hbm, first_hbm, second_hbm, third_hbm, w_hbm,
    out_hbm, ig_hbm, gg_hbm, first_hbm_grad, second_hbm_grad, third_hbm_grad,
    out_ref, ig_ref, gg_ref, first_grad, second_grad, third_grad,
    tok_ref, cot_ref, first_ref, second_ref, third_ref, w_ref,
    tok_all, tok_t, pair_out, pair_in, across_out, across_in, input_part,
    first_out, first_in, grad_out, grad_in, mixed_out, mixed_in, back_out, back_in,
    second_val, gate_a, gate_a_in, gate_b, gate_b_in, gate_a2, gate_a2_in, gate_b2, gate_b2_in,
    gate_x, gate_x_in, fg_out, fg_in, fg_ch, fg_fin, fg_ref, st_x, st_ch, st_fin, st_ref, st_rows,
    send_sem, recv_sem, load_sem, store_sem, y_sem, x_sem,
):
    me = lax.axis_index(SEQ)
    ch = lax.axis_index("ch")
    far, half = me // 2, lax.rem(me, 2)
    row, group = me // 4, lax.rem(me, 4)
    at_z, at_y = me // 16, lax.rem(me // 2, 8)
    chip, core = ch // 2, lax.rem(ch, 2)
    sibling = chip * 2 + 1 - core
    across = (1 - chip) * 2 + core
    corner = (1 - chip) * 2 + 1 - core

    def copy(kind, src, dst, where):
        pltpu.make_async_remote_copy(
            src, dst, send_sem.at[kind], recv_sem.at[kind],
            device_id=where, device_id_type=pl.DeviceIdType.MESH,
        ).start()

    def greet(sem, where):
        pl.semaphore_signal(sem, inc=1, device_id=where, device_id_type=pl.DeviceIdType.MESH)

    def received(kind, part):
        pltpu.make_async_copy(part, part, recv_sem.at[kind]).wait()

    def sent(kind, part):
        pltpu.make_async_copy(part, part, send_sem.at[kind]).wait()

    def to_seq(kind, src, dst, first=1, last=N):
        def step(d, carry):
            peer = lax.rem(me + d, N)
            copy(kind, src(peer), dst, place(peer))
            return carry

        lax.fori_loop(first, last, step, 0)

    def to_ch(kind, src, dst):
        for d in (1, 2, 3):
            peer = lax.rem(ch + d, 4)
            copy(kind, src(peer), dst, {"ch": peer})

    def share(kind, buffer):
        copy(kind + 1, buffer.at[ch], buffer.at[ch], {"ch": across})
        copy(kind, buffer.at[ch], buffer.at[ch], {"ch": sibling})

    def pass_on(kind, buffer):
        received(kind + 1, buffer.at[across])
        copy(kind + 2, buffer.at[across], buffer.at[across], {"ch": sibling})

    barrier = pltpu.get_barrier_semaphore()
    for d in range(1, 8):
        greet(barrier, {"seq_0": lax.rem(at_z + d, 8)})
        greet(barrier, {"seq_1": lax.rem(at_y + d, 8)})
    greet(barrier, {"seq_2": 1 - half})
    for d in (1, 2, 3):
        greet(barrier, {"ch": lax.rem(ch + d, 4)})
    loads = [
        pltpu.make_async_copy(src, dst, load_sem.at[n])
        for n, (src, dst) in enumerate(
            (
                (tok_hbm, tok_ref), (first_hbm, first_ref), (second_hbm, second_ref),
                (third_hbm, third_ref), (cot_hbm, cot_ref), (w_hbm, w_ref),
            )
        )
    ]
    for load in loads:
        load.start()
    stores = [
        pltpu.make_async_copy(src, dst, store_sem.at[n])
        for n, (src, dst) in enumerate(
            (
                (out_ref, out_hbm), (ig_ref, ig_hbm), (gg_ref, gg_hbm),
                (first_grad, first_hbm_grad), (second_grad, second_hbm_grad), (third_grad, third_hbm_grad),
            )
        )
    ]

    square = (256, 256)
    r, k = index(square, 0), index(square, 1)
    to_far = one_hot(k == (r & 3) * 64 + (r >> 2))
    to_home = one_hot(k == (r & 63) * 4 + (r >> 6))
    loads[0].wait()
    tok_all[ch] = nn(to_far, tok_ref[...]).astype(BF)
    loads[1].wait()
    spread_d = one_hot((index((64, 256), 1) & 63) == index((64, 256), 0))
    first_big = nn(jnp.concatenate([first_ref[group * 4 + b] for b in range(4)], axis=0), spread_d)
    first_big = jnp.where((r >> 6) == (k >> 6), first_big, 0.0).astype(BF)
    first_mat = nn(nn(to_far, first_big).astype(BF), to_home).astype(BF)
    first_back = nn(nt(to_far, first_big).astype(BF), to_home).astype(BF)

    def split_columns(values, buffer):
        for h in range(2):
            buffer[h] = values[:, h * 128 : h * 128 + 128].reshape(C, 4, 128)

    def join_columns(buffer):
        return jnp.concatenate([buffer[h].reshape(256, 128) for h in range(2)], axis=1)

    split_columns(nn(first_mat, tok_all[ch]).astype(BF), first_out)
    first_in[me] = first_out[half, far]

    rows32 = one_hot((index((512, 32), 0) >> 4) == index((512, 32), 1))
    rows16 = one_hot((index((256, 16), 0) & 15) == index((256, 16), 1))
    same_a = (r >> 4) == (k >> 4)
    same_b = (index((512, 512), 0) & 15) == (index((512, 512), 1) & 15)

    def own(ref, size):
        shape = (size, size, C)
        return jnp.sum(jnp.where(index(shape, 2) == far, ref[...].astype(F32), 0.0), axis=2).astype(BF)

    def spread_third(t):
        return jnp.where(same_b, nt(t.astype(BF), rows32), 0.0).astype(BF)

    def spread_second(t):
        return jnp.where(same_a, nt(t.astype(BF), rows16), 0.0).astype(BF)

    def w_rows(p):
        return w_ref[pl.ds(pl.multiple_of(p * 256, 256), 256), :]

    def gate_term(p):
        return nn(tok_all[p], w_rows(p))

    pl.semaphore_wait(barrier, 18)

    share(TOK, tok_all)
    for d in range(1, 8):
        greet(y_sem, {"seq_1": lax.rem(at_y + d, 8)})
    loads[2].wait()
    own_second = own(second_ref, B)
    second_mat = spread_second(nn(rows16, own_second))
    second_back = spread_second(nt(rows16, own_second))
    pl.semaphore_wait(y_sem, 7)
    greet(x_sem, {"seq_2": 1 - half})
    loads[3].wait()
    own_third = own(third_ref, A)
    third_mat, third_back = spread_third(nn(rows32, own_third)), spread_third(nt(rows32, own_third))
    loads[4].wait()
    upstream = nn(to_far, cot_ref[...])
    loads[5].wait()
    gate = gate_term(ch)
    pl.semaphore_wait(x_sem, 1)

    def first_for(peer):
        return first_out.at[lax.rem(peer, 2), peer // 2]

    to_seq(FIRST, first_for, first_in.at[me], 1, 64)
    pass_on(TOK, tok_all)
    to_seq(FIRST, first_for, first_in.at[me], 64, N)

    received(TOK, tok_all.at[sibling])
    gate += gate_term(sibling) + gate_term(across)
    received(TOK_LAST, tok_all.at[0])
    gate += gate_term(corner)
    sigmoid = jax.nn.sigmoid(gate)
    activation = gate * sigmoid
    split_columns((upstream * activation).astype(BF), grad_out)
    grad_in[me] = grad_out[half, far]
    to_seq(GRAD, lambda peer: grad_out.at[lax.rem(peer, 2), peer // 2], grad_in.at[me])

    received(FIRST, first_in.at[pl.ds(0, N - 1)])
    far_first = first_in[...].reshape(512, 128)
    for h in range(2):
        second_val[h * 256 : h * 256 + 256, :] = nn(second_mat, far_first[h * 256 : h * 256 + 256]).astype(BF)
    mixed_out[...] = nn(third_mat, second_val[...]).astype(BF).reshape(N, 4, 128)
    mixed_in[half, far] = mixed_out[me]
    to_seq(MIXED, lambda peer: mixed_out.at[peer], mixed_in.at[half, far])
    for p in range(4):
        tok_t[p] = tok_all[p].T

    received(GRAD, grad_in.at[pl.ds(0, N - 1)])
    far_grad = grad_in[...].reshape(512, 128)
    back_second = nn(third_back, far_grad).astype(BF)
    back_first = jnp.concatenate(
        [nn(second_back, back_second[h * 256 : h * 256 + 256]).astype(BF) for h in range(2)], axis=0
    )
    back_out[...] = back_first.reshape(N, 4, 128)
    back_in[half, far] = back_out[me]
    to_seq(BACK, lambda peer: back_out.at[peer], back_in.at[half, far])

    received(MIXED, first_in.at[pl.ds(0, N - 1)])
    mixed = join_columns(mixed_in).astype(F32)
    pre_grad = (upstream * mixed * sigmoid * (1.0 + gate * (1.0 - sigmoid))).astype(BF)
    for p in range(4):
        term = nn(tok_t[p], pre_grad)
        gate_a[2 * p : 2 * p + 2] = term[:, 0:128].reshape(2, 128, 128).astype(BF)
        for n in range(16):
            gate_b[n % 8, 2 * p + n // 8] = term[n * 16 : n * 16 + 16, 128:256].astype(BF)
    gate_a_in[at_z] = gate_a[at_z]
    gate_b_in[at_y] = gate_b[at_y]
    for d in range(1, 8):
        peer_z, peer_y = lax.rem(at_z + d, 8), lax.rem(at_y + d, 8)
        copy(GATE_A, gate_a.at[peer_z], gate_a_in.at[at_z], {"seq_0": peer_z})
        copy(GATE_B, gate_b.at[peer_y], gate_b_in.at[at_y], {"seq_1": peer_y})

    pair_out[0] = nt(pre_grad, w_rows(sibling)).astype(BF)
    pair_out[1] = nt(pre_grad, w_rows(corner)).astype(BF)
    copy(PAIR, pair_out, pair_in, {"ch": sibling})
    input_part[0] = nt(pre_grad, w_rows(ch))
    input_part[1] = nt(pre_grad, w_rows(across))

    third_part = jnp.where(same_b, nt(far_grad, second_val[...]), 0.0)
    third_part = summed(jnp.sum(third_part.reshape(A, B, 512), axis=1), rows32)
    second_part = jnp.zeros((16, 256), F32)
    for h in range(2):
        rows = slice(h * 256, h * 256 + 256)
        term = jnp.where(same_a, nt(back_second[rows], far_first[rows]), 0.0)
        second_part += jnp.sum(term.reshape(16, 16, 256), axis=0)
    second_part = summed(second_part, rows16)
    st_x[0] = jnp.concatenate(
        [
            jnp.concatenate([third_part[n * 8 : n * 8 + 8] for n in range(4)], axis=1),
            jnp.concatenate([second_part[0:8], second_part[8:16], jnp.zeros((8, 96), F32)], axis=1),
        ],
        axis=0,
    )
    copy(ST_X, st_x.at[0], st_x.at[1], {"seq_2": 1 - half})
    received(PAIR, pair_in)
    across_out[...] = (input_part[1] + pair_in[1].astype(F32)).astype(BF)
    copy(ACROSS, across_out, across_in, {"ch": across})

    received(BACK, grad_in.at[pl.ds(0, N - 1)])
    back_home = join_columns(back_in)
    first_part = jnp.where((r & 3) == (k & 3), nt(back_home, tok_all[ch]), 0.0)
    first_part = summed(first_part, one_hot((index((256, 64), 0) >> 2) == index((256, 64), 1)))
    fg_out[...] = jnp.concatenate([first_part[0:128], first_part[128:256]], axis=1).reshape(32, 4, 128)
    fg_in[row] = fg_out[row]

    def to_rows(d, carry):
        peer = lax.rem(row + d, 32)
        copy(FG_SUM, fg_out.at[peer], fg_in.at[row], place(peer * 4 + group))
        return carry

    lax.fori_loop(1, 32, to_rows, 0)

    received(ST_X, st_x.at[1])
    st_ch[ch] = st_x[0] + st_x[1]
    to_ch(ST_CH, lambda peer: st_ch.at[ch], st_ch.at[ch])

    received(GATE_A, gate_a_in.at[pl.ds(0, 7)])
    gate_a2[...] = jnp.sum(gate_a_in[...].astype(F32), axis=0).astype(BF).reshape(8, 16, 128)
    received(GATE_B, gate_b_in.at[pl.ds(0, 7)])
    gate_b2[...] = jnp.sum(gate_b_in[...].astype(F32), axis=0).astype(BF)
    gate_a2_in[at_y] = gate_a2[at_y]
    gate_b2_in[at_z] = gate_b2[at_z]
    for d in range(1, 8):
        peer_z, peer_y = lax.rem(at_z + d, 8), lax.rem(at_y + d, 8)
        copy(GATE_A2, gate_a2.at[peer_y], gate_a2_in.at[at_y], {"seq_1": peer_y})
        copy(GATE_B2, gate_b2.at[peer_z], gate_b2_in.at[at_z], {"seq_0": peer_z})

    received(FG_SUM, fg_in.at[pl.ds(0, 31)])
    fg_ch[ch] = jnp.sum(fg_in[...], axis=0)
    to_ch(FG_CH, lambda peer: fg_ch.at[ch], fg_ch.at[ch])

    received(ST_CH, st_ch.at[pl.ds(0, 3)])
    st_fin[...] = (st_ch[0] + st_ch[1] + st_ch[2] + st_ch[3]).astype(BF)
    st_ref[far] = st_fin[...]

    def to_columns(d, carry):
        peer = lax.rem(far + d, 64)
        copy(ST_ALL, st_fin, st_ref.at[far], place(peer * 2 + half))
        return carry

    lax.fori_loop(1, 64, to_columns, 0)

    received(FG_CH, fg_ch.at[pl.ds(0, 3)])
    fg_fin[...] = (fg_ch[0] + fg_ch[1] + fg_ch[2] + fg_ch[3]).astype(BF)
    fg_ref[me] = fg_fin[...]
    to_seq(FG_ALL, lambda peer: fg_fin, fg_ref.at[me])

    received(GATE_A2, gate_a2_in.at[pl.ds(0, 7)])
    received(GATE_B2, gate_b2_in.at[pl.ds(0, 7)])
    gate_sum = jnp.concatenate(
        [jnp.sum(part[...].astype(F32), axis=0) for part in (gate_a2_in, gate_b2_in)], axis=1
    )
    gate_x[0] = gate_sum[0:8]
    gate_x[1] = gate_sum[8:16]
    copy(GATE_X, gate_x.at[1 - half], gate_x_in, {"seq_2": 1 - half})

    out_ref[...] = nn(to_home, (tok_all[ch].astype(F32) + mixed * activation).astype(BF)).astype(BF)
    stores[0].start()
    received(ACROSS, across_in)
    in_grad = upstream + nn(first_back, back_home) + input_part[0]
    in_grad += pair_in[0].astype(F32) + across_in[...].astype(F32)
    ig_ref[...] = nn(to_home, in_grad.astype(BF)).astype(BF)
    stores[1].start()
    received(GATE_X, gate_x_in)
    gg_ref[...] = gate_x[half] + gate_x_in[...]
    stores[2].start()

    by_part = one_hot(k == (r & 15) * 16 + (r >> 4))
    by_block = one_hot(
        index((512, 512), 1) == (index((512, 512), 0) & 31) * 16 + (index((512, 512), 0) >> 5)
    )
    eye = one_hot(index((128, 128), 0) == index((128, 128), 1))
    received(ST_ALL, st_ref.at[pl.ds(0, 63)])
    for g in range(4):
        block = st_ref[g * 16 : g * 16 + 16].reshape(256, 128)
        st_rows[:, g * 16 : g * 16 + 16, :] = nn(by_part, block).astype(BF).reshape(16, 16, 128)
    for n in range(8):
        turned = nt(eye, st_rows[n]).astype(BF)
        for m in range(4):
            third_grad[m * 8 + n] = turned[m * 32 : m * 32 + 32]
    stores[5].start()
    for n in range(8):
        turned = nt(eye[0:32], st_rows[8 + n]).astype(BF)
        for m in range(2):
            second_grad[m * 8 + n] = turned[m * 16 : m * 16 + 16]
    stores[4].start()
    received(FG_ALL, fg_ref.at[pl.ds(0, N - 1)])
    blocks = nn(by_block, fg_ref[...].reshape(512, 128)).astype(BF).reshape(B, 32, 128)
    for h in range(2):
        first_grad[:, h * 32 : h * 32 + 32, :] = blocks[:, :, h * 64 : h * 64 + 64]
    stores[3].start()

    for kind, part in (
        (TOK, tok_all.at[0]),
        (TOK_FAR, tok_all.at[0]),
        (TOK_LAST, tok_all.at[0]),
        (FIRST, first_in.at[pl.ds(0, N - 1)]),
        (GRAD, grad_in.at[pl.ds(0, N - 1)]),
        (MIXED, first_in.at[pl.ds(0, N - 1)]),
        (BACK, first_in.at[pl.ds(0, N - 1)]),
        (PAIR, pair_out),
        (ACROSS, across_out),
        (GATE_A, gate_a_in.at[pl.ds(0, 7)]),
        (GATE_B, gate_b_in.at[pl.ds(0, 7)]),
        (GATE_A2, gate_a2_in.at[pl.ds(0, 7)]),
        (GATE_B2, gate_b2_in.at[pl.ds(0, 7)]),
        (GATE_X, gate_x_in),
        (FG_SUM, fg_in.at[pl.ds(0, 31)]),
        (FG_CH, fg_ch.at[pl.ds(0, 3)]),
        (FG_ALL, fg_ref.at[pl.ds(0, N - 1)]),
        (ST_X, st_x.at[0]),
        (ST_CH, st_ch.at[pl.ds(0, 3)]),
        (ST_ALL, st_ref.at[pl.ds(0, 63)]),
    ):
        sent(kind, part)
    for store in stores:
        store.wait()


def copies(*refs):
    sources, results, held = refs[0:6], refs[6:12], refs[12:18]
    load_sem, store_sem = refs[18:20]
    loads = [pltpu.make_async_copy(sources[n], held[n], load_sem.at[n]) for n in range(6)]
    stores = [pltpu.make_async_copy(held[n], results[n], store_sem.at[n]) for n in range(6)]
    for load in loads:
        load.start()
    for load, store in zip(loads, stores):
        load.wait()
        store.start()
    for store in stores:
        store.wait()


def on_device(tokens, cotangent, first_factor, second_factor, third_factor, gate_weight):
    vm = pltpu.VMEM
    anywhere = pl.BlockSpec(memory_space=pl.ANY)
    shapes = (
        jax.ShapeDtypeStruct((256, 256), BF),
        jax.ShapeDtypeStruct((256, 256), BF),
        jax.ShapeDtypeStruct((8, 256), F32),
        jax.ShapeDtypeStruct((B, C, C), BF),
        jax.ShapeDtypeStruct((B, B, C), BF),
        jax.ShapeDtypeStruct((A, A, C), BF),
    )
    results = pl.pallas_call(
        kernel,
        out_shape=shapes,
        in_specs=[anywhere] * 6,
        out_specs=[anywhere] * 6,
        scratch_shapes=[
            *[vm(shape.shape, shape.dtype) for shape in shapes],
            vm((256, 256), BF),
            vm((256, 256), BF),
            vm((B, C, C), BF),
            vm((B, B, C), BF),
            vm((A, A, C), BF),
            vm((1024, 256), BF),
            *[vm((4, 256, 256), BF)] * 2,
            *[vm((2, 256, 256), BF)] * 2,
            *[vm((256, 256), BF)] * 2,
            vm((2, 256, 256), F32),
            vm((2, C, 4, 128), BF),
            vm((N, 4, 128), BF),
            vm((2, C, 4, 128), BF),
            vm((N, 4, 128), BF),
            vm((N, 4, 128), BF),
            vm((2, C, 4, 128), BF),
            vm((N, 4, 128), BF),
            vm((2, C, 4, 128), BF),
            vm((512, 128), BF),
            *[vm((8, 128, 128), BF)] * 2,
            *[vm((8, 8, 16, 128), BF)] * 2,
            *[vm((8, 16, 128), BF)] * 4,
            vm((2, 8, 256), F32),
            vm((8, 256), F32),
            vm((32, 4, 128), F32),
            vm((32, 4, 128), F32),
            vm((4, 4, 128), F32),
            vm((4, 128), BF),
            vm((N, 4, 128), BF),
            vm((2, 16, 128), F32),
            vm((4, 16, 128), F32),
            vm((16, 128), BF),
            vm((C, 16, 128), BF),
            vm((16, C, 128), BF),
            pltpu.SemaphoreType.DMA((20,)),
            pltpu.SemaphoreType.DMA((20,)),
            pltpu.SemaphoreType.DMA((6,)),
            pltpu.SemaphoreType.DMA((6,)),
            pltpu.SemaphoreType.REGULAR,
            pltpu.SemaphoreType.REGULAR,
        ],
        compiler_params=pltpu.CompilerParams(
            collective_id=0, has_side_effects=True, vmem_limit_bytes=56 * 1024 * 1024
        ),
    )(
        tokens,
        cotangent,
        first_factor,
        second_factor.transpose(1, 2, 0),
        third_factor.transpose(1, 2, 0),
        gate_weight,
    )
    output, input_grad, gate_grad, first, second, third = pl.pallas_call(
        copies,
        out_shape=shapes,
        in_specs=[anywhere] * 6,
        out_specs=[anywhere] * 6,
        scratch_shapes=[
            *[vm(shape.shape, shape.dtype) for shape in shapes],
            pltpu.SemaphoreType.DMA((6,)),
            pltpu.SemaphoreType.DMA((6,)),
        ],
    )(*results)
    return output, input_grad, first, second.transpose(2, 0, 1), third.transpose(2, 0, 1), gate_grad


def solution(mesh):
    torus = Mesh(mesh.devices.reshape(8, 8, 2, mesh.shape["ch"]), (*SEQ, "ch"))
    return jax.shard_map(
        on_device,
        mesh=torus,
        in_specs=(P(SEQ, "ch"), P(SEQ, "ch"), P(), P(), P(), P(None, "ch")),
        out_specs=(P(SEQ, "ch"), P(SEQ, "ch"), P(), P(), P(), P(SEQ, "ch")),
        check_vma=False,
    )
```
